256 devices in a mesh: ctx: 16 (over x, y_lo, core), head: 16 (over y_hi, z).
Axes of the slice: x: 4, y: 4 (y_hi: 2, y_lo: 2; y = y_hi * 2 + y_lo), z: 8, core: 2. Of those that a mesh axis runs over, the one named last changes fastest.
Arguments:
- query_rows: bfloat16 [6144, 12288], P('ctx', 'head'), may hold values from -100 to 100
- key_rows: bfloat16 [6144, 1024], P('ctx', 'head'), may hold values from -5 to 5
- value_rows: bfloat16 [6144, 1024], P('ctx', 'head'), may hold values from -6 to 6
- block_order: int32 [32], P('ctx'), may hold values from 0 to 31, as said below
- rollout_ids: int32 [6144], P('ctx'), may hold values from 0 to 3, as said below
Outputs:
- attended: bfloat16 [6144, 12288], P('ctx', 'head')
The draws below stay inside these ranges and needn't reach their ends.
Inputs may be any that keep to these rules, and one draw needn't show every extreme that they name: `block_order`: each of 0 to 31 appears exactly once. `rollout_ids`: rollout numbers never fall as positions rise; the last position carries 4 - 1.
All inputs are finite; a program needn't handle non-finite values.
Results may differ from the reference program's by a relative error of at most 0.01.
Values may be sent and summed in bfloat16 or wider, within the bound.
A program may use at most 128 MiB of HBM per device.

```python
import jax
import jax.numpy as jnp
from jax import lax

QH = 96
KVH = 8
DH = 128
TOK_DEV = 384
SEGS = 4
SEQ = 6144
BLOCKS = 32
N_CTX = 16


def shared_order(key):
    return jax.random.permutation(jax.random.fold_in(key, 201), BLOCKS).astype(jnp.int32)


def base_keys(key):
    return jnp.clip(jax.random.normal(jax.random.fold_in(key, 301), (SEQ, KVH * DH), jnp.float32), -5.0, 5.0)


def draw_block_order(key, part):
    order = shared_order(key)
    return order


def draw_rollout_ids(key, part):
    order = shared_order(key)
    key = jax.random.fold_in(key, 2)
    cuts = jax.random.randint(key, (SEGS - 1,), 1, SEQ)
    stored = jnp.arange(SEQ, dtype=jnp.int32)
    half_rows = TOK_DEV // 2
    positions = jnp.take(order, stored // half_rows) * half_rows + stored % half_rows
    return jnp.sum((positions[:, None] >= cuts[None, :]).astype(jnp.int32), axis=1).astype(jnp.int32)


def draw_key_rows(key, part):
    base = base_keys(key)
    return base.astype(jnp.bfloat16)


def draw_query_rows(key, part):
    key = jax.random.fold_in(key, 4)
    values = 2.5 * jnp.clip(jax.random.normal(key, (SEQ, QH * DH), jnp.float32), -5.0, 5.0)
    return values.astype(jnp.bfloat16)


def shard_levels(rng, shape, cuts, smallest, high):
    def one(axis_at, parts):
        steps = jax.random.uniform(jax.random.fold_in(jax.random.fold_in(rng, 6), axis_at), (parts,), jnp.float32, smallest / len(cuts), high / len(cuts))
        return jnp.repeat(jnp.exp(steps), shape[axis_at] // parts).reshape((-1,) + (1,) * (len(shape) - axis_at - 1))

    level = one(*cuts[0])
    for cut in cuts[1:]:
        level = level * one(*cut)
    return level


def centred(key, extent, scale, bound, pieces=(), held_as=jnp.bfloat16):
    entries = scale * jax.random.normal(key, extent, jnp.float32)
    if pieces:
        entries = entries * shard_levels(key, extent, pieces, -0.22, 0.18)
    return jnp.clip(entries, -bound, bound).astype(held_as)


def setup_inputs(seed: int = 0) -> dict:
    seeds = jax.random.split(jax.random.key(seed), 6)
    query_rows = draw_query_rows(jax.random.fold_in(seeds[5], 71), 0)
    key_rows = draw_key_rows(jax.random.fold_in(seeds[5], 71), 0)
    value_rows = centred(seeds[2], (SEQ, KVH * DH), 1.0, 6.0, ((0, 16), (1, 16)))
    block_order = draw_block_order(jax.random.fold_in(seeds[5], 71), 0)
    rollout_ids = draw_rollout_ids(jax.random.fold_in(seeds[5], 71), 0)
    return dict(query_rows=query_rows, key_rows=key_rows, value_rows=value_rows, block_order=block_order, rollout_ids=rollout_ids)


NEG = -1.0e30


def group_partial(query_grp, query_pos, query_ids, key_blk, value_blk, key_pos, key_ids):
    allowed = (key_pos[None, :] <= query_pos[:, None]) & (key_ids[None, :] == query_ids[:, None])
    scores = jnp.einsum("qhd,kd->hqk", query_grp.astype(jnp.float32), key_blk.astype(jnp.float32)) * (DH ** -0.5)
    scores = jnp.where(allowed[None], scores, NEG)
    highest = jnp.max(scores, axis=-1)
    weights = jnp.where(allowed[None], jnp.exp(scores - highest[..., None]), 0.0)
    totals = jnp.sum(weights, axis=-1)
    rounded = lax.optimization_barrier(weights.astype(jnp.bfloat16)).astype(jnp.float32)
    mixed = jnp.einsum("hqk,kd->qhd", rounded, value_blk.astype(jnp.float32))
    safe_tot = jnp.where(totals > 0, totals, 1.0)
    part_out = (mixed / jnp.transpose(safe_tot, (1, 0))[..., None]).astype(jnp.bfloat16)
    log_sum = jnp.where(totals > 0, highest + jnp.log(safe_tot), NEG)
    return part_out, jnp.transpose(log_sum, (1, 0))


def reference(query_rows, key_rows, value_rows, block_order, rollout_ids):
    group_size = QH // KVH
    half_rows = TOK_DEV // 2
    stored = jnp.arange(SEQ, dtype=jnp.int32)
    positions = (jnp.take(block_order, stored // half_rows) * half_rows + stored % half_rows).astype(jnp.int32)
    query_split = jnp.transpose(query_rows.reshape(SEQ, KVH, group_size, DH), (1, 0, 2, 3))
    key_split = jnp.transpose(key_rows.reshape(SEQ, KVH, DH), (1, 0, 2))
    value_split = jnp.transpose(value_rows.reshape(SEQ, KVH, DH), (1, 0, 2))

    def one_group(operands):
        query_grp, key_grp, value_grp = operands

        def absorb(carry, block_index):
            run_max, numerator, denominator = carry
            start_row = (block_index * TOK_DEV).astype(jnp.int32)
            key_blk = lax.dynamic_slice_in_dim(key_grp, start_row, TOK_DEV, 0)
            value_blk = lax.dynamic_slice_in_dim(value_grp, start_row, TOK_DEV, 0)
            key_pos = lax.dynamic_slice_in_dim(positions, start_row, TOK_DEV, 0)
            key_ids = lax.dynamic_slice_in_dim(rollout_ids, start_row, TOK_DEV, 0)
            part_out, log_sum = group_partial(query_grp, positions, rollout_ids, key_blk, value_blk, key_pos, key_ids)
            newest = jnp.maximum(run_max, log_sum)
            fading = jnp.exp(run_max - newest)
            weight = jnp.exp(log_sum - newest)
            numerator = numerator * fading[..., None] + weight[..., None] * part_out.astype(jnp.float32)
            denominator = denominator * fading + weight
            return (newest, numerator, denominator), None

        initial = (jnp.full((SEQ, group_size), NEG, jnp.float32),
                   jnp.zeros((SEQ, group_size, DH), jnp.float32),
                   jnp.zeros((SEQ, group_size), jnp.float32))
        (run_max, numerator, denominator), ignored = lax.scan(absorb, initial, jnp.arange(N_CTX, dtype=jnp.int32))
        return (numerator / denominator[..., None]).astype(jnp.bfloat16)

    merged = lax.map(one_group, (query_split, key_split, value_split))
    return jnp.transpose(merged, (1, 0, 2, 3)).reshape(SEQ, QH * DH)
```

```python
import jax
import jax.numpy as jnp
from jax import lax
from jax.experimental import pallas as pl
from jax.experimental.pallas import tpu as pltpu
from jax.sharding import PartitionSpec as P

MESH = pl.DeviceIdType.MESH
N_CTX = 16
RING = 4
DIM2 = (0, -1, 1, 2)


def gather_kernel(own_ref, ids_ref, k_ref, v_ref, slots, plan_ref,
                  mine, meta, send_sem, recv_sem, sib_send, sib_recv, meta_send, meta_recv, keep_sem):
    rows = k_ref.shape[1]
    half = rows // 2
    ctx = lax.axis_index("ctx")
    head = lax.axis_index("head")
    core = ctx % 2
    x = ctx // 4
    y = ctx // 2 % 2
    z = head % 2
    base = head - z
    r = y + z * (3 - 2 * y)
    a = x + core * (r - x)
    b = r + core * (x - r)

    def locate(pa, pb, which):
        pa = (pa + 2 * RING) % RING
        pb = (pb + 2 * RING) % RING
        px = pa + which * (pb - pa)
        pr = pb + which * (pa - pb)
        pz = pr // 2
        py = (pr + pz) % 2
        return px * 4 + py * 2 + which, pz

    def device(pa, pb, which):
        c, pz = locate(pa, pb, which)
        return (c, base + pz)

    def slot(pa, pb, which):
        c, pz = locate(pa, pb, which)
        return c * 2 + pz

    barrier = pltpu.get_barrier_semaphore()
    for step in range(1, N_CTX):
        pl.semaphore_signal(barrier, inc=1, device_id=((ctx + step) % N_CTX, head), device_id_type=MESH)
    for there in (ctx, ctx + 2 - 4 * y):
        pl.semaphore_signal(barrier, inc=1, device_id=(there, base + 1 - z), device_id_type=MESH)

    mine[...] = jnp.concatenate([k_ref[...], v_ref[...]], axis=0).T
    lane = lax.broadcasted_iota(jnp.int32, (8, 128), 1)
    sub = lax.broadcasted_iota(jnp.int32, (8, 128), 0)
    tile = jnp.where(lane == 0, own_ref[0], own_ref[1])
    for t in range(3):
        tile = jnp.where(sub == t + 1, jnp.broadcast_to(ids_ref[t:t + 1, :], (8, 128)), tile)
    meta[ctx] = tile
    keep = pltpu.make_async_copy(mine, slots.at[slot(a, b, core)], keep_sem)
    keep.start()
    pl.semaphore_wait(barrier, N_CTX + 1)

    started = []
    spans = {"all": pl.ds(0, rows), "low": pl.ds(0, half), "high": pl.ds(half, half)}

    def copy(index, da, db, part, ua, ub):
        here = slots.at[slot(a + da, b + db, core), spans[part]]
        src = mine if (da == 0 and db == 0) else here
        return pltpu.make_async_remote_copy(
            src_ref=src, dst_ref=here, send_sem=send_sem.at[index], recv_sem=recv_sem.at[index],
            device_id=device(a + ua, b + ub, core), device_id_type=MESH)

    def arrive(index, da, db, part, ua, ub):
        there = slots.at[slot(a + da - ua, b + db - ub, core), spans[part]]
        pltpu.make_async_remote_copy(
            src_ref=there, dst_ref=there, send_sem=send_sem.at[index], recv_sem=recv_sem.at[index],
            device_id=device(a + ua, b + ub, core), device_id_type=MESH).wait_recv()

    kinds = {}

    def kind(name, *what):
        kinds[name] = (len(kinds),) + what

    kind("a+", 0, 0, "all", 1, 0)
    kind("a-", 0, 0, "all", -1, 0)
    kind("a2", 0, 0, "all", 2, 0)
    for da in DIM2:
        kind(("+", da), da, 0, "all", 0, 1)
        kind(("-", da), da, 0, "all", 0, -1)
        if da != 2:
            kind(("++", da), da, -1, "low", 0, 1)
            kind(("--", da), da, 1, "high", 0, -1)
        else:
            kind(("2", da), da, 0, "all", 0, 2)

    def send(name):
        cp = copy(*kinds[name])
        cp.start()
        started.append(cp)

    def wait(name):
        arrive(*kinds[name])

    def sib(index, da, db, other):
        if other:
            here = slots.at[slot(b + da, a + db, 1 - core)]
            src = here
        else:
            here = slots.at[slot(a + da, b + db, core)]
            src = mine if (da == 0 and db == 0) else here
        return pltpu.make_async_remote_copy(
            src_ref=src, dst_ref=here, send_sem=sib_send.at[index], recv_sem=sib_recv.at[index],
            device_id=(ctx + 1 - 2 * core, head), device_id_type=MESH)

    shared = []

    def share(da, db):
        index = len(shared)
        shared.append((index, da, db))
        cp = sib(index, da, db, False)
        cp.start()
        started.append(cp)

    def out(da):
        send(("+", da))
        send(("-", da))
        if da == 2:
            send(("2", da))

    def metas():
        for step in range(1, N_CTX):
            cp = pltpu.make_async_remote_copy(
                src_ref=meta.at[ctx], dst_ref=meta.at[ctx], send_sem=meta_send.at[step], recv_sem=meta_recv.at[step],
                device_id=((ctx + step) % N_CTX, head), device_id_type=MESH)
            cp.start()
            started.append(cp)

    send("a+")
    send("a-")
    send("a2")
    share(0, 0)
    metas()
    out(0)
    wait("a+")
    wait("a-")
    for da in (-1, 1):
        out(da)
        share(da, 0)
    wait("a2")
    out(2)
    share(2, 0)
    for da in DIM2:
        wait(("+", da))
        if da != 2:
            send(("++", da))
        wait(("-", da))
        if da != 2:
            send(("--", da))
        share(da, -1)
        share(da, 1)
    for da in DIM2:
        if da != 2:
            wait(("++", da))
            wait(("--", da))
        else:
            wait(("2", da))
        share(da, 2)

    for step in range(1, N_CTX):
        src = (ctx + N_CTX - step) % N_CTX
        pltpu.make_async_remote_copy(
            src_ref=meta.at[src], dst_ref=meta.at[src], send_sem=meta_send.at[step], recv_sem=meta_recv.at[step],
            device_id=(src, head), device_id_type=MESH).wait_recv()
    everything = meta[...]
    plan_ref[0:16, :] = everything[:, 0, :]
    ids = everything[:, 1:4, :]
    for cut in range(3):
        count = jnp.sum((ids <= cut).astype(jnp.int32), axis=(0, 1)).reshape(1, 128)
        plan_ref[16 + cut:17 + cut, :] = jnp.broadcast_to(jnp.sum(count, axis=1, keepdims=True), (1, 128))
    plan_ref[19:24, :] = jnp.zeros((5, 128), jnp.int32)

    for index, da, db in shared:
        sib(index, da, db, True).wait_recv()
    keep.wait()
    for cp in started:
        cp.wait_send()


def gather(own, ids, k, v):
    rows = k.shape[0]
    vm = pl.BlockSpec(memory_space=pltpu.VMEM)
    sm = pl.BlockSpec(memory_space=pltpu.SMEM)
    n = 4 + 4 * len(DIM2)
    return pl.pallas_call(
        gather_kernel,
        out_shape=(jax.ShapeDtypeStruct((2 * N_CTX, rows, 128), jnp.bfloat16),
                   jax.ShapeDtypeStruct((24, 128), jnp.int32)),
        in_specs=[sm, vm, vm, vm],
        out_specs=(pl.BlockSpec(memory_space=pl.ANY), vm),
        scratch_shapes=[
            pltpu.VMEM((rows, 128), jnp.bfloat16),
            pltpu.VMEM((N_CTX, 8, 128), jnp.int32),
            pltpu.SemaphoreType.DMA((n,)),
            pltpu.SemaphoreType.DMA((n,)),
            pltpu.SemaphoreType.DMA((16,)),
            pltpu.SemaphoreType.DMA((16,)),
            pltpu.SemaphoreType.DMA((N_CTX,)),
            pltpu.SemaphoreType.DMA((N_CTX,)),
            pltpu.SemaphoreType.DMA(()),
        ],
        compiler_params=pltpu.CompilerParams(collective_id=0, has_side_effects=True),
        name="gather",
    )(own, ids.reshape(3, 128), k.T, v.T)


DH = 128
HALF = 192
NBLK = 32
SEQ = 6144
C = 512
LOG2E = 1.4426950408889634
SCALE = DH ** -0.5 * LOG2E
NEG = -1e30
LIMIT = 2.0 ** 100
NT = (((1,), (1,)), ((), ()))


def attend_kernel(own_ref, plan_ref, q_ref, slots, o_ref,
                  stage, ks, vs, acc, tot, mx, inv, sem):
    heads = q_ref.shape[1] // DH

    def place(c, _):
        inv[plan_ref[c, 0]] = 2 * c
        inv[plan_ref[c, 1]] = 2 * c + 1
        return 0

    lax.fori_loop(0, NBLK // 2, place, 0)
    cuts = [plan_ref[16 + cut, 0] for cut in range(3)]

    def start_of(pos):
        lo = jnp.int32(0)
        for cut in cuts:
            lo = jnp.where(cut <= pos, jnp.maximum(lo, cut), lo)
        return lo

    def spans(i):
        first = own_ref[i] * HALF
        lo0 = start_of(first)
        lo1 = start_of(first + HALF - 1)
        j0 = lo0 // C
        j3 = (first + HALF - 1) // C + 1
        j2 = jnp.maximum((first + 1) // C, j0)
        j1 = jnp.minimum((lo1 + C - 1) // C, j2)
        return first, lo0, lo1, j0, j1, j2, j3, (j0 * C) // HALF, (j3 * C - 1) // HALF

    s0 = spans(0)
    s1 = spans(1)

    def copies(p):
        src = pl.ds(pl.multiple_of(inv[p] % 2 * HALF, HALF), HALF)
        dst = pl.ds(pl.multiple_of(p * HALF, HALF), HALF)
        return [pltpu.make_async_copy(slots.at[inv[p] // 2 * 2 + z, src], stage.at[z, dst], sem.at[z, p])
                for z in range(2)]

    def assemble(p):
        for cp in copies(p):
            cp.wait()
        at = pl.ds(pl.multiple_of(p * HALF, HALF), HALF)
        ks[at, :64] = stage[0, at, :64]
        ks[at, 64:] = stage[1, at, :64]
        vs[at, :64] = stage[0, at, 64:]
        vs[at, 64:] = stage[1, at, 64:]

    def in0(p):
        return (p >= s0[7]) & (p <= s0[8])

    def start(p, _):
        for cp in copies(p):
            cp.start()
        return 0

    def start1(p, _):
        @pl.when(jnp.logical_not(in0(p)))
        def _():
            for cp in copies(p):
                cp.start()
        return 0

    lax.fori_loop(s0[7], s0[8] + 1, start, 0)
    lax.fori_loop(s1[7], s1[8] + 1, start1, 0)

    def wait0(p, _):
        assemble(p)
        return 0

    def wait1(p, _):
        @pl.when(jnp.logical_not(in0(p)))
        def _():
            assemble(p)
        return 0

    def allowed_for(first, lo_rows, j):
        kpos = j * C + lax.broadcasted_iota(jnp.int32, (HALF, C), 1)
        qpos = first + lax.broadcasted_iota(jnp.int32, (HALF, C), 0)
        return (kpos <= qpos) & (kpos >= lo_rows)

    def rows_start(first):
        qpos = first + lax.broadcasted_iota(jnp.int32, (HALF, C), 0)
        lo = jnp.zeros((HALF, C), jnp.int32)
        for cut in cuts:
            lo = jnp.where(cut <= qpos, jnp.maximum(lo, cut), lo)
        return lo

    for i in range(2):
        first, lo0, lo1, j0, j1, j2, j3, plo, phi = s1 if i else s0
        lax.fori_loop(plo, phi + 1, wait1 if i else wait0, 0)
        rows = slice(i * HALF, (i + 1) * HALF)
        kself = ks[pl.ds(pl.multiple_of(first, HALF), HALF), :].astype(jnp.float32)
        for h in range(heads):
            qh = q_ref[rows, h * DH:(h + 1) * DH].astype(jnp.float32)
            m = jnp.sum(qh * kself, axis=1, keepdims=True) * SCALE
            mx[h] = jnp.broadcast_to(m, (HALF, DH))
            acc[h] = jnp.zeros((HALF, DH), jnp.float32)
            tot[h] = jnp.zeros((HALF, DH), jnp.float32)
        lo_rows = rows_start(first)

        def step(j, masked):
            at = pl.ds(pl.multiple_of(j * C, C), C)
            k = ks[at, :]
            v = vs[at, :]
            if masked:
                allowed = allowed_for(first, lo_rows, j)

            def scores(h):
                return lax.dot_general(q_ref[rows, h * DH:(h + 1) * DH], k, NT,
                                       preferred_element_type=jnp.float32)

            nxt = scores(0)
            for h in range(heads):
                s = nxt
                if h + 1 < heads:
                    nxt = scores(h + 1)
                m = mx[h]
                s = s * SCALE - jnp.concatenate([m] * (C // DH), axis=1)
                if masked:
                    s = jnp.where(allowed, s, NEG)
                p = jnp.exp2(s)
                t = tot[h]
                for part in range(C // DH):
                    t = t + p[:, part * DH:(part + 1) * DH]
                tot[h] = t
                acc[h] += jnp.dot(p.astype(jnp.bfloat16), v, preferred_element_type=jnp.float32)

        def edge(t, _):
            step(jnp.where(t < j1 - j0, j0 + t, j2 + t - (j1 - j0)), True)
            return 0

        def inner(j, _):
            step(j, False)
            return 0

        lax.fori_loop(0, (j1 - j0) + (j3 - j2), edge, 0)
        lax.fori_loop(j1, j2, inner, 0)

        worst = jnp.float32(0)
        for h in range(heads):
            t = jnp.sum(tot[h], axis=1, keepdims=True)
            worst = jnp.maximum(worst, jnp.max(t))
            o_ref[rows, h * DH:(h + 1) * DH] = (acc[h] / t).astype(jnp.bfloat16)

        @pl.when(jnp.logical_not(worst < LIMIT))
        def _():
            def one(h, _):
                cols = pl.ds(pl.multiple_of(h * DH, DH), DH)
                q = q_ref[rows, cols]

                def safe(j, carry):
                    top, total, mixed = carry
                    at = pl.ds(pl.multiple_of(j * C, C), C)
                    s = lax.dot_general(q, ks[at, :], NT, preferred_element_type=jnp.float32) * SCALE
                    ok = allowed_for(first, lo_rows, j)
                    s = jnp.where(ok, s, NEG)
                    new = jnp.maximum(top, jnp.max(s, axis=1, keepdims=True))
                    p = jnp.where(ok, jnp.exp2(s - new), 0.0)
                    fade = jnp.exp2(top - new)
                    total = total * fade + jnp.sum(p, axis=1, keepdims=True)
                    mixed = mixed * fade + jnp.dot(p.astype(jnp.bfloat16), vs[at, :],
                                                   preferred_element_type=jnp.float32)
                    return new, total, mixed

                top, total, mixed = lax.fori_loop(
                    j0, j3, safe,
                    (jnp.full((HALF, 1), NEG, jnp.float32), jnp.zeros((HALF, 1), jnp.float32),
                     jnp.zeros((HALF, DH), jnp.float32)))
                o_ref[rows, cols] = (mixed / total).astype(jnp.bfloat16)
                return 0

            lax.fori_loop(0, heads, one, 0)


def attend(own, plan, q, slots):
    heads = q.shape[1] // DH
    vm = pl.BlockSpec(memory_space=pltpu.VMEM)
    sm = pl.BlockSpec(memory_space=pltpu.SMEM)
    anym = pl.BlockSpec(memory_space=pl.ANY)
    return pl.pallas_call(
        attend_kernel,
        out_shape=jax.ShapeDtypeStruct(q.shape, jnp.bfloat16),
        in_specs=[sm, sm, vm, anym],
        out_specs=vm,
        scratch_shapes=[
            pltpu.VMEM((2, SEQ, DH), jnp.bfloat16),
            pltpu.VMEM((SEQ, DH), jnp.bfloat16),
            pltpu.VMEM((SEQ, DH), jnp.bfloat16),
            pltpu.VMEM((heads, HALF, DH), jnp.float32),
            pltpu.VMEM((heads, HALF, DH), jnp.float32),
            pltpu.VMEM((heads, HALF, DH), jnp.float32),
            pltpu.SMEM((NBLK,), jnp.int32),
            pltpu.SemaphoreType.DMA((2, NBLK)),
        ],
        compiler_params=pltpu.CompilerParams(vmem_limit_bytes=48 * 2**20),
        name="attend",
    )(own, plan, q, slots)


def per_device(query_rows, key_rows, value_rows, block_order, rollout_ids):
    slots, plan = gather(block_order, rollout_ids, key_rows, value_rows)
    return attend(block_order, plan, query_rows, slots)


def solution(mesh):
    return jax.shard_map(
        per_device,
        mesh=mesh,
        in_specs=(P("ctx", "head"), P("ctx", "head"), P("ctx", "head"), P("ctx"), P("ctx")),
        out_specs=P("ctx", "head"),
        check_vma=False,
    )
```

```python
import jax
import jax.numpy as jnp
from jax import lax
from jax.experimental import pallas as pl
from jax.experimental.pallas import tpu as pltpu
from jax.sharding import PartitionSpec as P

MESH = pl.DeviceIdType.MESH
N_CTX = 16
RING = 4
DIM2 = (0, -1, 1, 2)


def gather_kernel(own_hbm, ids_hbm, k_hbm, v_hbm, ka_ref, va_ref, plan_ref,
                  slots, raw, own_ref, ids_ref, load_sem, mine, meta, send_sem, recv_sem, sib_send, sib_recv, meta_send, meta_recv, keep_sem):
    rows = k_hbm.shape[1]
    half = rows // 2
    ctx = lax.axis_index("ctx")
    head = lax.axis_index("head")
    core = ctx % 2
    x = ctx // 4
    y = ctx // 2 % 2
    z = head % 2
    base = head - z
    r = y + z * (3 - 2 * y)
    a = x + core * (r - x)
    b = r + core * (x - r)

    def locate(pa, pb, which):
        pa = (pa + 2 * RING) % RING
        pb = (pb + 2 * RING) % RING
        px = pa + which * (pb - pa)
        pr = pb + which * (pa - pb)
        pz = pr // 2
        py = (pr + pz) % 2
        return px * 4 + py * 2 + which, pz

    def device(pa, pb, which):
        c, pz = locate(pa, pb, which)
        return (c, base + pz)

    def slot(pa, pb, which):
        c, pz = locate(pa, pb, which)
        return c * 2 + pz

    loads = [pltpu.make_async_copy(k_hbm, raw.at[pl.ds(0, 64)], load_sem.at[0]),
             pltpu.make_async_copy(v_hbm, raw.at[pl.ds(64, 64)], load_sem.at[1]),
             pltpu.make_async_copy(own_hbm, own_ref, load_sem.at[2]),
             pltpu.make_async_copy(ids_hbm, ids_ref, load_sem.at[3])]
    for cp in loads:
        cp.start()

    barrier = pltpu.get_barrier_semaphore()
    for step in range(1, N_CTX):
        pl.semaphore_signal(barrier, inc=1, device_id=((ctx + step) % N_CTX, head), device_id_type=MESH)
    for there in (ctx, ctx + 2 - 4 * y):
        pl.semaphore_signal(barrier, inc=1, device_id=(there, base + 1 - z), device_id_type=MESH)

    for cp in loads:
        cp.wait()
    mine[...] = raw[...].T
    lane = lax.broadcasted_iota(jnp.int32, (8, 128), 1)
    sub = lax.broadcasted_iota(jnp.int32, (8, 128), 0)
    tile = jnp.where(lane == 0, own_ref[0], own_ref[1])
    for t in range(3):
        tile = jnp.where(sub == t + 1, jnp.broadcast_to(ids_ref[t:t + 1, :], (8, 128)), tile)
    meta[ctx] = tile
    keep = pltpu.make_async_copy(mine, slots.at[slot(a, b, core)], keep_sem)
    keep.start()
    pl.semaphore_wait(barrier, N_CTX + 1)

    started = []
    spans = {"all": pl.ds(0, rows), "low": pl.ds(0, half), "high": pl.ds(half, half)}

    def copy(index, da, db, part, ua, ub):
        here = slots.at[slot(a + da, b + db, core), spans[part]]
        src = mine if (da == 0 and db == 0) else here
        return pltpu.make_async_remote_copy(
            src_ref=src, dst_ref=here, send_sem=send_sem.at[index], recv_sem=recv_sem.at[index],
            device_id=device(a + ua, b + ub, core), device_id_type=MESH)

    def arrive(index, da, db, part, ua, ub):
        there = slots.at[slot(a + da - ua, b + db - ub, core), spans[part]]
        pltpu.make_async_remote_copy(
            src_ref=there, dst_ref=there, send_sem=send_sem.at[index], recv_sem=recv_sem.at[index],
            device_id=device(a + ua, b + ub, core), device_id_type=MESH).wait_recv()

    kinds = {}

    def kind(name, *what):
        kinds[name] = (len(kinds),) + what

    kind("a+", 0, 0, "all", 1, 0)
    kind("a-", 0, 0, "all", -1, 0)
    kind("a2", 0, 0, "all", 2, 0)
    for da in DIM2:
        kind(("+", da), da, 0, "all", 0, 1)
        kind(("-", da), da, 0, "all", 0, -1)
        if da != 2:
            kind(("++", da), da, -1, "low", 0, 1)
            kind(("--", da), da, 1, "high", 0, -1)
        else:
            kind(("2", da), da, 0, "all", 0, 2)

    def send(name):
        cp = copy(*kinds[name])
        cp.start()
        started.append(cp)

    def wait(name):
        arrive(*kinds[name])

    def sib(index, da, db, other):
        if other:
            here = slots.at[slot(b + da, a + db, 1 - core)]
            src = here
        else:
            here = slots.at[slot(a + da, b + db, core)]
            src = mine if (da == 0 and db == 0) else here
        return pltpu.make_async_remote_copy(
            src_ref=src, dst_ref=here, send_sem=sib_send.at[index], recv_sem=sib_recv.at[index],
            device_id=(ctx + 1 - 2 * core, head), device_id_type=MESH)

    shared = []

    def share(da, db):
        index = len(shared)
        shared.append((index, da, db))
        cp = sib(index, da, db, False)
        cp.start()
        started.append(cp)

    def out(da):
        send(("+", da))
        send(("-", da))
        if da == 2:
            send(("2", da))

    def metas():
        for step in range(1, N_CTX):
            cp = pltpu.make_async_remote_copy(
                src_ref=meta.at[ctx], dst_ref=meta.at[ctx], send_sem=meta_send.at[step], recv_sem=meta_recv.at[step],
                device_id=((ctx + step) % N_CTX, head), device_id_type=MESH)
            cp.start()
            started.append(cp)

    send("a+")
    send("a-")
    send("a2")
    share(0, 0)
    metas()
    out(0)
    wait("a+")
    wait("a-")
    for da in (-1, 1):
        out(da)
        share(da, 0)
    wait("a2")
    out(2)
    share(2, 0)
    for da in DIM2:
        wait(("+", da))
        if da != 2:
            send(("++", da))
        wait(("-", da))
        if da != 2:
            send(("--", da))
        share(da, -1)
        share(da, 1)
    for da in DIM2:
        if da != 2:
            wait(("++", da))
            wait(("--", da))
        else:
            wait(("2", da))
        share(da, 2)

    def assemble(place, which):
        c = place * 2 + which
        at = pl.ds(pl.multiple_of(c * rows, rows), rows)
        low = slots[2 * c]
        high = slots[2 * c + 1]
        ka_ref[at, :] = jnp.concatenate([low[:, :64], high[:, :64]], axis=1)
        va_ref[at, :] = jnp.concatenate([low[:, 64:], high[:, 64:]], axis=1)

    keep.wait()
    for place in range(N_CTX // 2):
        assemble(place, core)
    for step in range(1, N_CTX):
        src = (ctx + N_CTX - step) % N_CTX
        pltpu.make_async_remote_copy(
            src_ref=meta.at[src], dst_ref=meta.at[src], send_sem=meta_send.at[step], recv_sem=meta_recv.at[step],
            device_id=(src, head), device_id_type=MESH).wait_recv()
    everything = meta[...]
    plan_ref[0:16, :] = everything[:, 0, :]
    ids = everything[:, 1:4, :]
    for cut in range(3):
        count = jnp.sum((ids <= cut).astype(jnp.int32), axis=(0, 1)).reshape(1, 128)
        plan_ref[16 + cut:17 + cut, :] = jnp.broadcast_to(jnp.sum(count, axis=1, keepdims=True), (1, 128))
    plan_ref[19:24, :] = jnp.zeros((5, 128), jnp.int32)

    for index, da, db in shared:
        sib(index, da, db, True).wait_recv()
    for place in range(N_CTX // 2):
        assemble(place, 1 - core)
    for cp in started:
        cp.wait_send()


def gather(own, ids, k, v):
    rows = k.shape[0]
    vm = pl.BlockSpec(memory_space=pltpu.VMEM)
    hbm = pl.BlockSpec(memory_space=pltpu.HBM)
    n = 3 + 2 * len(DIM2) + 2 * (len(DIM2) - 1) + 1
    every = jax.ShapeDtypeStruct((N_CTX * rows, 128), jnp.bfloat16)
    return pl.pallas_call(
        gather_kernel,
        out_shape=(every, every, jax.ShapeDtypeStruct((24, 128), jnp.int32)),
        in_specs=[hbm, hbm, hbm, hbm],
        out_specs=(vm, vm, vm),
        scratch_shapes=[
            pltpu.VMEM((2 * N_CTX, rows, 128), jnp.bfloat16),
            pltpu.VMEM((128, rows), jnp.bfloat16),
            pltpu.SMEM((2,), jnp.int32),
            pltpu.VMEM((3, 128), jnp.int32),
            pltpu.SemaphoreType.DMA((4,)),
            pltpu.VMEM((rows, 128), jnp.bfloat16),
            pltpu.VMEM((N_CTX, 8, 128), jnp.int32),
            pltpu.SemaphoreType.DMA((n,)),
            pltpu.SemaphoreType.DMA((n,)),
            pltpu.SemaphoreType.DMA((16,)),
            pltpu.SemaphoreType.DMA((16,)),
            pltpu.SemaphoreType.DMA((N_CTX,)),
            pltpu.SemaphoreType.DMA((N_CTX,)),
            pltpu.SemaphoreType.DMA(()),
        ],
        compiler_params=pltpu.CompilerParams(
            collective_id=0, has_side_effects=True, vmem_limit_bytes=24 * 2**20),
        name="gather",
    )(*(pltpu.with_memory_space_constraint(x, pltpu.HBM) for x in (own, ids.reshape(3, 128), k.T, v.T)))


DH = 128
HALF = 192
NBLK = 32
SEQ = 6144
LOG2E = 1.4426950408889634
SCALE = DH ** -0.5 * LOG2E
NEG = -1e30
LIMIT = 2.0 ** 100
WIDE = 4
EDGE = 2
NT = (((1,), (1,)), ((), ()))


def attend_kernel(own_hbm, plan_ref, q_hbm, k_ref, v_ref, o_ref,
                  q_ref, acc, tot, mx, own_ref, inv, sem):
    heads = q_ref.shape[1] // DH
    q_copy = pltpu.make_async_copy(q_hbm, q_ref, sem.at[0])
    q_copy.start()
    own_copy = pltpu.make_async_copy(own_hbm, own_ref, sem.at[1])
    own_copy.start()

    def place(c, _):
        inv[plan_ref[c, 0]] = 2 * c
        inv[plan_ref[c, 1]] = 2 * c + 1
        return 0

    lax.fori_loop(0, NBLK // 2, place, 0)
    cuts = [plan_ref[16 + cut, 0] for cut in range(3)]
    own_copy.wait()
    q_copy.wait()

    def start_of(pos):
        lo = jnp.zeros_like(pos)
        for cut in cuts:
            lo = jnp.where(cut <= pos, jnp.maximum(lo, cut), lo)
        return lo

    def rows_of(p):
        return pl.ds(pl.multiple_of(inv[p] * HALF, HALF), HALF)

    def gathered(ref, blocks):
        return jnp.concatenate([ref[rows_of(p), :] for p in blocks], axis=0)

    for i in range(2):
        block = own_ref[i]
        first = block * HALF
        lo0 = start_of(first)
        lo1 = start_of(first + HALF - 1)
        head = lo0 // HALF
        body = jnp.clip((lo1 + HALF - 1) // HALF, head, block)
        spare = (block - body) % WIDE
        body = body + spare
        n_edge = body - head + 1
        rows = slice(i * HALF, (i + 1) * HALF)
        kself = k_ref[rows_of(block), :].astype(jnp.float32)
        for h in range(heads):
            qh = q_ref[rows, h * DH:(h + 1) * DH].astype(jnp.float32)
            m = jnp.sum(qh * kself, axis=1, keepdims=True) * SCALE
            mx[h] = jnp.broadcast_to(m, (HALF, DH))
            acc[h] = jnp.zeros((HALF, DH), jnp.float32)
            tot[h] = jnp.zeros((HALF, DH), jnp.float32)
        qpos = first + lax.broadcasted_iota(jnp.int32, (HALF, HALF), 0)
        lo_rows = start_of(qpos)
        lane = lax.broadcasted_iota(jnp.int32, (HALF, HALF), 1)
        wide_qpos = first + lax.broadcasted_iota(jnp.int32, (HALF, EDGE * HALF), 0)
        wide_lo = start_of(wide_qpos)
        wide_lane = lax.broadcasted_iota(jnp.int32, (HALF, EDGE * HALF), 1)

        def edge_blocks(t):
            index = [EDGE * t + e for e in range(EDGE)]
            blocks = [jnp.where(at < n_edge - 1, head + at, block) for at in index]
            kpos = None
            for e, (at, p) in enumerate(zip(index, blocks)):
                here = jnp.where(at < n_edge, p * HALF - HALF * e, SEQ) + wide_lane
                kpos = here if kpos is None else jnp.where(wide_lane < HALF * e, kpos, here)
            return blocks, (kpos <= wide_qpos) & (kpos >= wide_lo)

        def step(blocks, allowed):
            k = gathered(k_ref, blocks)
            v = gathered(v_ref, blocks)
            wide = HALF * len(blocks)

            def scores(h):
                return lax.dot_general(q_ref[rows, h * DH:(h + 1) * DH], k, NT,
                                       preferred_element_type=jnp.float32)

            nxt = scores(0)
            for h in range(heads):
                s = nxt
                if h + 1 < heads:
                    nxt = scores(h + 1)
                s = s * SCALE - jnp.concatenate([mx[h]] * (wide // DH), axis=1)
                if allowed is not None:
                    s = jnp.where(allowed, s, NEG)
                p = jnp.exp2(s)
                t = tot[h]
                for part in range(wide // DH):
                    t = t + p[:, part * DH:(part + 1) * DH]
                tot[h] = t
                acc[h] += jnp.dot(p.astype(jnp.bfloat16), v, preferred_element_type=jnp.float32)

        def edge(t, _):
            step(*edge_blocks(t))
            return 0

        def inner(t, _):
            step([body + WIDE * t + e for e in range(WIDE)], None)
            return 0

        n_steps = (n_edge + EDGE - 1) // EDGE
        lax.fori_loop(0, n_steps, edge, 0)
        lax.fori_loop(0, (block - body) // WIDE, inner, 0)

        worst = None
        for h in range(heads):
            t = jnp.sum(tot[h], axis=1, keepdims=True)
            worst = t if worst is None else jnp.maximum(worst, t)
            o_ref[rows, h * DH:(h + 1) * DH] = (acc[h] * (1.0 / t)).astype(jnp.bfloat16)

        @pl.when(jnp.logical_not(jnp.max(worst) < LIMIT))
        def _():
            def one(h, _):
                cols = pl.ds(pl.multiple_of(h * DH, DH), DH)
                q = q_ref[rows, cols]

                def safe(p, carry):
                    top, total, mixed = carry
                    s = lax.dot_general(q, k_ref[rows_of(p), :], NT, preferred_element_type=jnp.float32) * SCALE
                    kpos = p * HALF + lane
                    ok = (kpos <= qpos) & (kpos >= lo_rows)
                    s = jnp.where(ok, s, NEG)
                    new = jnp.maximum(top, jnp.max(s, axis=1, keepdims=True))
                    w = jnp.where(ok, jnp.exp2(s - new), 0.0)
                    fade = jnp.exp2(top - new)
                    total = total * fade + jnp.sum(w, axis=1, keepdims=True)
                    mixed = mixed * fade + jnp.dot(w.astype(jnp.bfloat16), v_ref[rows_of(p), :],
                                                   preferred_element_type=jnp.float32)
                    return new, total, mixed

                top, total, mixed = lax.fori_loop(
                    head, block + 1, safe,
                    (jnp.full((HALF, 1), NEG, jnp.float32), jnp.zeros((HALF, 1), jnp.float32),
                     jnp.zeros((HALF, DH), jnp.float32)))
                o_ref[rows, cols] = (mixed / total).astype(jnp.bfloat16)
                return 0

            lax.fori_loop(0, heads, one, 0)


def attend(own, plan, q, k, v):
    heads = q.shape[1] // DH
    vm = pl.BlockSpec(memory_space=pltpu.VMEM)
    sm = pl.BlockSpec(memory_space=pltpu.SMEM)
    hbm = pl.BlockSpec(memory_space=pltpu.HBM)
    return pl.pallas_call(
        attend_kernel,
        out_shape=jax.ShapeDtypeStruct(q.shape, jnp.bfloat16),
        in_specs=[hbm, sm, hbm, vm, vm],
        out_specs=vm,
        scratch_shapes=[
            pltpu.VMEM(q.shape, jnp.bfloat16),
            pltpu.VMEM((heads, HALF, DH), jnp.float32),
            pltpu.VMEM((heads, HALF, DH), jnp.float32),
            pltpu.VMEM((heads, HALF, DH), jnp.float32),
            pltpu.SMEM((2,), jnp.int32),
            pltpu.SMEM((NBLK,), jnp.int32),
            pltpu.SemaphoreType.DMA((2,)),
        ],
        compiler_params=pltpu.CompilerParams(vmem_limit_bytes=32 * 2**20),
        name="attend",
    )(pltpu.with_memory_space_constraint(own, pltpu.HBM), plan,
      pltpu.with_memory_space_constraint(q, pltpu.HBM), k, v)


def per_device(query_rows, key_rows, value_rows, block_order, rollout_ids):
    keys, values, plan = gather(block_order, rollout_ids, key_rows, value_rows)
    return attend(block_order, plan, query_rows, keys, values)


def solution(mesh):
    return jax.shard_map(
        per_device,
        mesh=mesh,
        in_specs=(P("ctx", "head"), P("ctx", "head"), P("ctx", "head"), P("ctx"), P("ctx")),
        out_specs=P("ctx", "head"),
        check_vma=False,
    )
```

```python
import jax
import jax.numpy as jnp
from jax import lax
from jax.experimental import pallas as pl
from jax.experimental.pallas import tpu as pltpu
from jax.sharding import PartitionSpec as P

MESH = pl.DeviceIdType.MESH
N_CTX = 16
DIAG = 256
RING = 4
DIM2 = (0, -1, 1, 2)


def gather_kernel(own_hbm, ids_hbm, k_hbm, v_hbm, q_hbm, ka_ref, va_ref, plan_ref, q_ref, acc, tot, mx,
                  slots, raw, own_ref, ids_ref, load_sem, mine, meta, send_sem, recv_sem, sib_send, sib_recv, meta_send, meta_recv, keep_sem):
    rows = k_hbm.shape[1]
    half = rows // 2
    ctx = lax.axis_index("ctx")
    head = lax.axis_index("head")
    core = ctx % 2
    x = ctx // 4
    y = ctx // 2 % 2
    z = head % 2
    base = head - z
    r = y + z * (3 - 2 * y)
    a = x + core * (r - x)
    b = r + core * (x - r)

    def locate(pa, pb, which):
        pa = (pa + 2 * RING) % RING
        pb = (pb + 2 * RING) % RING
        px = pa + which * (pb - pa)
        pr = pb + which * (pa - pb)
        pz = pr // 2
        py = (pr + pz) % 2
        return px * 4 + py * 2 + which, pz

    def device(pa, pb, which):
        c, pz = locate(pa, pb, which)
        return (c, base + pz)

    def slot(pa, pb, which):
        c, pz = locate(pa, pb, which)
        return c * 2 + pz

    loads = [pltpu.make_async_copy(k_hbm, raw.at[pl.ds(0, 64)], load_sem.at[0]),
             pltpu.make_async_copy(v_hbm, raw.at[pl.ds(64, 64)], load_sem.at[1]),
             pltpu.make_async_copy(own_hbm, own_ref, load_sem.at[2]),
             pltpu.make_async_copy(ids_hbm, ids_ref, load_sem.at[3])]
    for cp in loads:
        cp.start()
    q_copy = pltpu.make_async_copy(q_hbm, q_ref, load_sem.at[4])
    q_copy.start()

    barrier = pltpu.get_barrier_semaphore()
    for step in range(1, N_CTX):
        pl.semaphore_signal(barrier, inc=1, device_id=((ctx + step) % N_CTX, head), device_id_type=MESH)
    for there in (ctx, ctx + 2 - 4 * y):
        pl.semaphore_signal(barrier, inc=1, device_id=(there, base + 1 - z), device_id_type=MESH)

    for cp in loads:
        cp.wait()
    mine[...] = raw[...].T
    lane = lax.broadcasted_iota(jnp.int32, (8, 128), 1)
    sub = lax.broadcasted_iota(jnp.int32, (8, 128), 0)
    tile = jnp.where(lane == 0, own_ref[0], own_ref[1])
    for t in range(3):
        tile = jnp.where(sub == t + 1, jnp.broadcast_to(ids_ref[t:t + 1, :], (8, 128)), tile)
    meta[ctx] = tile
    keep = pltpu.make_async_copy(mine, slots.at[slot(a, b, core)], keep_sem)
    keep.start()
    pl.semaphore_wait(barrier, N_CTX + 1)

    started = []
    spans = {"all": pl.ds(0, rows), "low": pl.ds(0, half), "high": pl.ds(half, half)}

    def copy(index, da, db, part, ua, ub):
        here = slots.at[slot(a + da, b + db, core), spans[part]]
        src = mine if (da == 0 and db == 0) else here
        return pltpu.make_async_remote_copy(
            src_ref=src, dst_ref=here, send_sem=send_sem.at[index], recv_sem=recv_sem.at[index],
            device_id=device(a + ua, b + ub, core), device_id_type=MESH)

    def arrive(index, da, db, part, ua, ub):
        there = slots.at[slot(a + da - ua, b + db - ub, core), spans[part]]
        pltpu.make_async_remote_copy(
            src_ref=there, dst_ref=there, send_sem=send_sem.at[index], recv_sem=recv_sem.at[index],
            device_id=device(a + ua, b + ub, core), device_id_type=MESH).wait_recv()

    kinds = {}

    def kind(name, *what):
        kinds[name] = (len(kinds),) + what

    kind("a+", 0, 0, "all", 1, 0)
    kind("a-", 0, 0, "all", -1, 0)
    kind("a2", 0, 0, "all", 2, 0)
    for da in DIM2:
        kind(("+", da), da, 0, "all", 0, 1)
        kind(("-", da), da, 0, "all", 0, -1)
        if da != 2:
            kind(("++", da), da, -1, "low", 0, 1)
            kind(("--", da), da, 1, "high", 0, -1)
        else:
            kind(("2", da), da, 0, "all", 0, 2)

    def send(name):
        cp = copy(*kinds[name])
        cp.start()
        started.append(cp)

    def wait(name):
        arrive(*kinds[name])

    def sib(index, da, db, other):
        if other:
            here = slots.at[slot(b + da, a + db, 1 - core)]
            src = here
        else:
            here = slots.at[slot(a + da, b + db, core)]
            src = mine if (da == 0 and db == 0) else here
        return pltpu.make_async_remote_copy(
            src_ref=src, dst_ref=here, send_sem=sib_send.at[index], recv_sem=sib_recv.at[index],
            device_id=(ctx + 1 - 2 * core, head), device_id_type=MESH)

    shared = []

    def share(da, db):
        index = len(shared)
        shared.append((index, da, db))
        cp = sib(index, da, db, False)
        cp.start()
        started.append(cp)

    def out(da):
        send(("+", da))
        send(("-", da))
        if da == 2:
            send(("2", da))

    def metas():
        for step in range(1, N_CTX):
            cp = pltpu.make_async_remote_copy(
                src_ref=meta.at[ctx], dst_ref=meta.at[ctx], send_sem=meta_send.at[step], recv_sem=meta_recv.at[step],
                device_id=((ctx + step) % N_CTX, head), device_id_type=MESH)
            cp.start()
            started.append(cp)

    send("a+")
    send("a-")
    send("a2")
    share(0, 0)
    metas()
    out(0)
    wait("a+")
    wait("a-")
    for da in (-1, 1):
        out(da)
        share(da, 0)
    wait("a2")
    out(2)
    share(2, 0)
    def spread(da):
        wait(("+", da))
        if da != 2:
            send(("++", da))
        wait(("-", da))
        if da != 2:
            send(("--", da))
        share(da, -1)
        share(da, 1)

    spread(0)
    for step in range(1, N_CTX):
        src = (ctx + N_CTX - step) % N_CTX
        pltpu.make_async_remote_copy(
            src_ref=meta.at[src], dst_ref=meta.at[src], send_sem=meta_send.at[step], recv_sem=meta_recv.at[step],
            device_id=(src, head), device_id_type=MESH).wait_recv()
    everything = meta[...]
    plan_ref[0:16, :] = everything[:, 0, :]
    ids = everything[:, 1:4, :]
    cuts = []
    for cut in range(3):
        count = jnp.sum((ids <= cut).astype(jnp.int32), axis=(0, 1)).reshape(1, 128)
        cuts.append(jnp.sum(count, axis=1, keepdims=True))
        plan_ref[16 + cut:17 + cut, :] = jnp.broadcast_to(cuts[cut], (1, 128))
    wide = lax.broadcasted_iota(jnp.int32, (16, 128), 1)
    twice = 2 * lax.broadcasted_iota(jnp.int32, (16, 128), 0)
    order = everything[:, 0, :]
    where = jnp.where(order[:, 0:1] == wide, twice, 0) + jnp.where(order[:, 1:2] == wide, twice + 1, 0)
    plan_ref[19:20, :] = jnp.sum(where, axis=0, keepdims=True)
    plan_ref[20:24, :] = jnp.zeros((4, 128), jnp.int32)


    keep.wait()
    q_copy.wait()
    low = slots[2 * ctx]
    high = slots[2 * ctx + 1]
    k_own = jnp.concatenate([low[:, :64], high[:, :64]], axis=1)
    v_own = jnp.concatenate([low[:, 64:], high[:, 64:]], axis=1)
    heads = q_ref.shape[1] // DH
    key = lax.broadcasted_iota(jnp.int32, (half, DIAG), 1)
    row = lax.broadcasted_iota(jnp.int32, (half, DIAG), 0)
    for i in range(2):
        begin = i * (rows - DIAG)
        first = own_ref[i] * half
        lo = jnp.zeros((half, DIAG), jnp.int32)
        for cut in cuts:
            lo = jnp.where(cut <= first + row, jnp.maximum(lo, cut), lo)
        at = key + begin - i * half
        allowed = (at >= 0) & (at <= row) & (first + at >= lo)
        k = k_own[begin:begin + DIAG]
        v = v_own[begin:begin + DIAG]
        k_self = k_own[i * half:(i + 1) * half].astype(jnp.float32)
        for h in range(heads):
            q = q_ref[i * half:(i + 1) * half, h * DH:(h + 1) * DH]
            m = jnp.sum(q.astype(jnp.float32) * k_self, axis=1, keepdims=True) * SCALE
            s = lax.dot_general(q, k, NT, preferred_element_type=jnp.float32) * SCALE - m
            p = jnp.exp2(jnp.where(allowed, s, NEG))
            mx[i * heads + h] = jnp.broadcast_to(m, (half, DH))
            tot[i * heads + h] = p[:, :DH] + p[:, DH:]
            acc[i * heads + h] = jnp.dot(p.astype(jnp.bfloat16), v, preferred_element_type=jnp.float32)

    for da in DIM2[1:]:
        spread(da)
    for da in DIM2:
        if da != 2:
            wait(("++", da))
            wait(("--", da))
        else:
            wait(("2", da))
        share(da, 2)

    def assemble(place, which):
        c = place * 2 + which
        at = pl.ds(pl.multiple_of(c * rows, rows), rows)
        low = slots[2 * c]
        high = slots[2 * c + 1]
        ka_ref[at, :] = jnp.concatenate([low[:, :64], high[:, :64]], axis=1)
        va_ref[at, :] = jnp.concatenate([low[:, 64:], high[:, 64:]], axis=1)

    for place in range(N_CTX // 2):
        assemble(place, core)
    for index, da, db in shared:
        sib(index, da, db, True).wait_recv()
    for place in range(N_CTX // 2):
        assemble(place, 1 - core)
    for cp in started:
        cp.wait_send()


def gather(own, ids, k, v, q):
    rows = k.shape[0]
    vm = pl.BlockSpec(memory_space=pltpu.VMEM)
    hbm = pl.BlockSpec(memory_space=pltpu.HBM)
    n = 3 + 2 * len(DIM2) + 2 * (len(DIM2) - 1) + 1
    every = jax.ShapeDtypeStruct((N_CTX * rows, 128), jnp.bfloat16)
    state = jax.ShapeDtypeStruct((2 * (q.shape[1] // DH), rows // 2, DH), jnp.float32)
    return pl.pallas_call(
        gather_kernel,
        out_shape=(every, every, jax.ShapeDtypeStruct((24, 128), jnp.int32),
                   jax.ShapeDtypeStruct(q.shape, q.dtype), state, state, state),
        in_specs=[hbm] * 5,
        out_specs=(vm,) * 7,
        scratch_shapes=[
            pltpu.VMEM((2 * N_CTX, rows, 128), jnp.bfloat16),
            pltpu.VMEM((128, rows), jnp.bfloat16),
            pltpu.SMEM((2,), jnp.int32),
            pltpu.VMEM((3, 128), jnp.int32),
            pltpu.SemaphoreType.DMA((5,)),
            pltpu.VMEM((rows, 128), jnp.bfloat16),
            pltpu.VMEM((N_CTX, 8, 128), jnp.int32),
            pltpu.SemaphoreType.DMA((n,)),
            pltpu.SemaphoreType.DMA((n,)),
            pltpu.SemaphoreType.DMA((16,)),
            pltpu.SemaphoreType.DMA((16,)),
            pltpu.SemaphoreType.DMA((N_CTX,)),
            pltpu.SemaphoreType.DMA((N_CTX,)),
            pltpu.SemaphoreType.DMA(()),
        ],
        compiler_params=pltpu.CompilerParams(
            collective_id=0, has_side_effects=True, vmem_limit_bytes=24 * 2**20),
        name="gather",
    )(*(pltpu.with_memory_space_constraint(x, pltpu.HBM) for x in (own, ids.reshape(3, 128), k.T, v.T, q)))


DH = 128
HALF = 192
NBLK = 32
SEQ = 6144
LOG2E = 1.4426950408889634
SCALE = DH ** -0.5 * LOG2E
NEG = -1e30
LIMIT = 2.0 ** 100
WIDE = 4
EDGE = 2
NT = (((1,), (1,)), ((), ()))


def attend_kernel(own_hbm, plan_ref, q_ref, k_ref, v_ref, acc_in, tot_in, mx_in, o_hbm,
                  acc, tot, o_ref, own_ref, sem):
    heads = q_ref.shape[1] // DH
    own_copy = pltpu.make_async_copy(own_hbm, own_ref, sem.at[2])
    own_copy.start()

    cuts = [plan_ref[16 + cut, 0] for cut in range(3)]
    own_copy.wait()

    def start_of(pos):
        lo = jnp.zeros_like(pos)
        for cut in cuts:
            lo = jnp.where(cut <= pos, jnp.maximum(lo, cut), lo)
        return lo

    def rows_of(p):
        return pl.ds(pl.multiple_of(plan_ref[19, p] * HALF, HALF), HALF)

    def gathered(ref, blocks):
        return jnp.concatenate([ref[rows_of(p), :] for p in blocks], axis=0)

    for i in range(2):
        block = own_ref[i]
        first = block * HALF
        lo0 = start_of(first)
        lo1 = start_of(first + HALF - 1)
        head = lo0 // HALF
        body = jnp.clip((lo1 + HALF - 1) // HALF, head, block)
        spare = (block - body) % WIDE
        body = body + spare
        n_edge = body - head
        rows = slice(i * HALF, (i + 1) * HALF)
        for h in range(heads):
            acc[h] = acc_in[i * heads + h]
            tot[h] = tot_in[i * heads + h]
        qpos = first + lax.broadcasted_iota(jnp.int32, (HALF, HALF), 0)
        lo_rows = start_of(qpos)
        lane = lax.broadcasted_iota(jnp.int32, (HALF, HALF), 1)
        wide_lo = start_of(first + lax.broadcasted_iota(jnp.int32, (HALF, EDGE * HALF), 0))
        wide_lane = lax.broadcasted_iota(jnp.int32, (HALF, EDGE * HALF), 1)

        def edge_blocks(t):
            index = [EDGE * t + e for e in range(EDGE)]
            blocks = [jnp.minimum(head + at, block) for at in index]
            kpos = None
            for e, (at, p) in enumerate(zip(index, blocks)):
                here = jnp.where(at < n_edge, p * HALF - HALF * e, -SEQ) + wide_lane
                kpos = here if kpos is None else jnp.where(wide_lane < HALF * e, kpos, here)
            return blocks, kpos >= wide_lo

        def step(blocks, allowed):
            k = gathered(k_ref, blocks)
            v = gathered(v_ref, blocks)
            wide = HALF * len(blocks)

            def scores(h):
                return lax.dot_general(q_ref[rows, h * DH:(h + 1) * DH], k, NT,
                                       preferred_element_type=jnp.float32)

            nxt = scores(0)
            for h in range(heads):
                s = nxt
                if h + 1 < heads:
                    nxt = scores(h + 1)
                s = s * SCALE - jnp.concatenate([mx_in[i * heads + h]] * (wide // DH), axis=1)
                if allowed is not None:
                    s = jnp.where(allowed, s, NEG)
                p = jnp.exp2(s)
                t = tot[h]
                for part in range(wide // DH):
                    t = t + p[:, part * DH:(part + 1) * DH]
                tot[h] = t
                acc[h] += jnp.dot(p.astype(jnp.bfloat16), v, preferred_element_type=jnp.float32)

        def edge(t, _):
            step(*edge_blocks(t))
            return 0

        def inner(t, _):
            step([body + WIDE * t + e for e in range(WIDE)], None)
            return 0

        n_steps = (n_edge + EDGE - 1) // EDGE
        lax.fori_loop(0, n_steps, edge, 0)
        lax.fori_loop(0, (block - body) // WIDE, inner, 0)

        worst = None
        for h in range(heads):
            t = jnp.sum(tot[h], axis=1, keepdims=True)
            worst = t if worst is None else jnp.maximum(worst, t)
            o_ref[rows, h * DH:(h + 1) * DH] = (acc[h] * (1.0 / t)).astype(jnp.bfloat16)

        @pl.when(jnp.logical_not(jnp.max(worst) < LIMIT))
        def _():
            def one(h, _):
                cols = pl.ds(pl.multiple_of(h * DH, DH), DH)
                q = q_ref[rows, cols]

                def safe(p, carry):
                    top, total, mixed = carry
                    s = lax.dot_general(q, k_ref[rows_of(p), :], NT, preferred_element_type=jnp.float32) * SCALE
                    kpos = p * HALF + lane
                    ok = (kpos <= qpos) & (kpos >= lo_rows)
                    s = jnp.where(ok, s, NEG)
                    new = jnp.maximum(top, jnp.max(s, axis=1, keepdims=True))
                    w = jnp.where(ok, jnp.exp2(s - new), 0.0)
                    fade = jnp.exp2(top - new)
                    total = total * fade + jnp.sum(w, axis=1, keepdims=True)
                    mixed = mixed * fade + jnp.dot(w.astype(jnp.bfloat16), v_ref[rows_of(p), :],
                                                   preferred_element_type=jnp.float32)
                    return new, total, mixed

                top, total, mixed = lax.fori_loop(
                    head, block + 1, safe,
                    (jnp.full((HALF, 1), NEG, jnp.float32), jnp.zeros((HALF, 1), jnp.float32),
                     jnp.zeros((HALF, DH), jnp.float32)))
                o_ref[rows, cols] = (mixed / total).astype(jnp.bfloat16)
                return 0

            lax.fori_loop(0, heads, one, 0)

        pltpu.make_async_copy(o_ref.at[rows], o_hbm.at[rows], sem.at[i]).start()

    for i in range(2):
        rows = slice(i * HALF, (i + 1) * HALF)
        pltpu.make_async_copy(o_ref.at[rows], o_hbm.at[rows], sem.at[i]).wait()


def attend(own, plan, q, k, v, acc, tot, mx):
    heads = q.shape[1] // DH
    vm = pl.BlockSpec(memory_space=pltpu.VMEM)
    sm = pl.BlockSpec(memory_space=pltpu.SMEM)
    hbm = pl.BlockSpec(memory_space=pltpu.HBM)
    return pl.pallas_call(
        attend_kernel,
        out_shape=jax.ShapeDtypeStruct(q.shape, jnp.bfloat16),
        in_specs=[hbm, sm] + [vm] * 6,
        out_specs=hbm,
        scratch_shapes=[
            pltpu.VMEM((heads, HALF, DH), jnp.float32),
            pltpu.VMEM((heads, HALF, DH), jnp.float32),
            pltpu.VMEM(q.shape, jnp.bfloat16),
            pltpu.SMEM((2,), jnp.int32),
            pltpu.SemaphoreType.DMA((3,)),
        ],
        compiler_params=pltpu.CompilerParams(vmem_limit_bytes=32 * 2**20),
        name="attend",
    )(pltpu.with_memory_space_constraint(own, pltpu.HBM), plan, q, k, v, acc, tot, mx)


def per_device(query_rows, key_rows, value_rows, block_order, rollout_ids):
    keys, values, plan, query, acc, tot, mx = gather(
        block_order, rollout_ids, key_rows, value_rows, query_rows)
    return attend(block_order, plan, query, keys, values, acc, tot, mx)


def solution(mesh):
    return jax.shard_map(
        per_device,
        mesh=mesh,
        in_specs=(P("ctx", "head"), P("ctx", "head"), P("ctx", "head"), P("ctx"), P("ctx")),
        out_specs=P("ctx", "head"),
        check_vma=False,
    )
```

```python
import jax
import jax.numpy as jnp
from jax import lax
from jax.experimental import pallas as pl
from jax.experimental.pallas import tpu as pltpu
from jax.sharding import PartitionSpec as P

MESH = pl.DeviceIdType.MESH
N_CTX = 16
DIAG = 256
WIDE = 4
RING = 4
DIM2 = (0, -1, 1, 2)


def gather_kernel(own_hbm, ids_hbm, k_hbm, v_hbm, q_hbm, ka_ref, va_ref, plan_ref, q_ref, acc, tot, mx,
                  slots, raw, own_ref, ids_ref, load_sem, mine, meta, send_sem, recv_sem, sib_send, sib_recv, meta_send, meta_recv, keep_sem):
    rows = k_hbm.shape[1]
    half = rows // 2
    ctx = lax.axis_index("ctx")
    head = lax.axis_index("head")
    core = ctx % 2
    x = ctx // 4
    y = ctx // 2 % 2
    z = head % 2
    base = head - z
    r = y + z * (3 - 2 * y)
    a = x + core * (r - x)
    b = r + core * (x - r)

    def locate(pa, pb, which):
        pa = (pa + 2 * RING) % RING
        pb = (pb + 2 * RING) % RING
        px = pa + which * (pb - pa)
        pr = pb + which * (pa - pb)
        pz = pr // 2
        py = (pr + pz) % 2
        return px * 4 + py * 2 + which, pz

    def device(pa, pb, which):
        c, pz = locate(pa, pb, which)
        return (c, base + pz)

    def slot(pa, pb, which):
        c, pz = locate(pa, pb, which)
        return c * 2 + pz

    barrier = pltpu.get_barrier_semaphore()
    for step in range(1, N_CTX):
        pl.semaphore_signal(barrier, inc=1, device_id=((ctx + step) % N_CTX, head), device_id_type=MESH)
    for there in (ctx, ctx + 2 - 4 * y):
        pl.semaphore_signal(barrier, inc=1, device_id=(there, base + 1 - z), device_id_type=MESH)

    loads = [pltpu.make_async_copy(k_hbm, raw.at[pl.ds(0, 64)], load_sem.at[0]),
             pltpu.make_async_copy(v_hbm, raw.at[pl.ds(64, 64)], load_sem.at[1]),
             pltpu.make_async_copy(own_hbm, own_ref, load_sem.at[2]),
             pltpu.make_async_copy(ids_hbm, ids_ref, load_sem.at[3])]
    for cp in loads:
        cp.start()
    q_copy = pltpu.make_async_copy(q_hbm, q_ref, load_sem.at[4])
    q_copy.start()

    for cp in loads:
        cp.wait()
    mine[...] = raw[...].T
    lane = lax.broadcasted_iota(jnp.int32, (8, 128), 1)
    sub = lax.broadcasted_iota(jnp.int32, (8, 128), 0)
    tile = jnp.where(lane == 0, own_ref[0], own_ref[1])
    for t in range(3):
        tile = jnp.where(sub == t + 1, jnp.broadcast_to(ids_ref[t:t + 1, :], (8, 128)), tile)
    meta[ctx] = tile
    keep = pltpu.make_async_copy(mine, slots.at[slot(a, b, core)], keep_sem)
    keep.start()
    pl.semaphore_wait(barrier, N_CTX + 1)

    started = []
    spans = {"all": pl.ds(0, rows), "low": pl.ds(0, half), "high": pl.ds(half, half)}

    def copy(index, da, db, part, ua, ub):
        here = slots.at[slot(a + da, b + db, core), spans[part]]
        src = mine if (da == 0 and db == 0) else here
        return pltpu.make_async_remote_copy(
            src_ref=src, dst_ref=here, send_sem=send_sem.at[index], recv_sem=recv_sem.at[index],
            device_id=device(a + ua, b + ub, core), device_id_type=MESH)

    def arrive(index, da, db, part, ua, ub):
        there = slots.at[slot(a + da - ua, b + db - ub, core), spans[part]]
        pltpu.make_async_remote_copy(
            src_ref=there, dst_ref=there, send_sem=send_sem.at[index], recv_sem=recv_sem.at[index],
            device_id=device(a + ua, b + ub, core), device_id_type=MESH).wait_recv()

    kinds = {}

    def kind(name, *what):
        kinds[name] = (len(kinds),) + what

    kind("a+", 0, 0, "all", 1, 0)
    kind("a-", 0, 0, "all", -1, 0)
    kind("a2", 0, 0, "all", 2, 0)
    for da in DIM2:
        kind(("+", da), da, 0, "all", 0, 1)
        kind(("-", da), da, 0, "all", 0, -1)
        if da != 2:
            kind(("++", da), da, -1, "low", 0, 1)
            kind(("--", da), da, 1, "high", 0, -1)
        else:
            kind(("2", da), da, 0, "all", 0, 2)

    def send(name):
        cp = copy(*kinds[name])
        cp.start()
        started.append(cp)

    def wait(name):
        arrive(*kinds[name])

    def sib(index, da, db, other):
        if other:
            here = slots.at[slot(b + da, a + db, 1 - core)]
            src = here
        else:
            here = slots.at[slot(a + da, b + db, core)]
            src = mine if (da == 0 and db == 0) else here
        return pltpu.make_async_remote_copy(
            src_ref=src, dst_ref=here, send_sem=sib_send.at[index], recv_sem=sib_recv.at[index],
            device_id=(ctx + 1 - 2 * core, head), device_id_type=MESH)

    shared = []

    def share(da, db):
        index = len(shared)
        shared.append((index, da, db))
        cp = sib(index, da, db, False)
        cp.start()
        started.append(cp)

    def out(da):
        send(("+", da))
        send(("-", da))
        if da == 2:
            send(("2", da))

    def metas():
        for step in range(1, N_CTX):
            cp = pltpu.make_async_remote_copy(
                src_ref=meta.at[ctx], dst_ref=meta.at[ctx], send_sem=meta_send.at[step], recv_sem=meta_recv.at[step],
                device_id=((ctx + step) % N_CTX, head), device_id_type=MESH)
            cp.start()
            started.append(cp)

    send("a+")
    send("a-")
    send("a2")
    share(0, 0)
    metas()
    out(0)
    wait("a+")
    wait("a-")
    for da in (-1, 1):
        out(da)
        share(da, 0)
    wait("a2")
    out(2)
    share(2, 0)
    def spread(da):
        wait(("+", da))
        if da != 2:
            send(("++", da))
        wait(("-", da))
        if da != 2:
            send(("--", da))
        share(da, -1)
        share(da, 1)

    spread(0)
    for step in range(1, N_CTX):
        src = (ctx + N_CTX - step) % N_CTX
        pltpu.make_async_remote_copy(
            src_ref=meta.at[src], dst_ref=meta.at[src], send_sem=meta_send.at[step], recv_sem=meta_recv.at[step],
            device_id=(src, head), device_id_type=MESH).wait_recv()
    everything = meta[...]
    plan_ref[0:16, :] = everything[:, 0, :]
    ids = everything[:, 1:4, :]
    cuts = []
    for cut in range(3):
        count = jnp.sum((ids <= cut).astype(jnp.int32), axis=(0, 1)).reshape(1, 128)
        cuts.append(jnp.sum(count, axis=1, keepdims=True))
        plan_ref[16 + cut:17 + cut, :] = jnp.broadcast_to(cuts[cut], (1, 128))
    wide = lax.broadcasted_iota(jnp.int32, (16, 128), 1)
    twice = 2 * lax.broadcasted_iota(jnp.int32, (16, 128), 0)
    order = everything[:, 0, :]
    where = jnp.where(order[:, 0:1] == wide, twice, 0) + jnp.where(order[:, 1:2] == wide, twice + 1, 0)
    stored = jnp.sum(where, axis=0, keepdims=True)
    plan_ref[19:20, :] = stored
    across = lax.broadcasted_iota(jnp.int32, (32, 128), 1)
    down = lax.broadcasted_iota(jnp.int32, (32, 128), 0)
    stored_wide = jnp.broadcast_to(stored, (32, 128))
    stored_col = jnp.sum(jnp.where(across == down, stored_wide, 0), axis=1, keepdims=True)

    def last_cut(pos):
        lo = jnp.zeros_like(pos)
        for cut in cuts:
            lo = jnp.where(cut <= pos, jnp.maximum(lo, cut), lo)
        return lo

    for i in range(2):
        first = own_ref[i] * half
        lo0 = last_cut(jnp.full((32, 128), first, jnp.int32))
        lo1 = last_cut(jnp.full((32, 128), first + half - 1, jnp.int32))

        def listed(p):
            return (p * half + half - 1 >= lo0) & (p * half < first) & (p < 2 * N_CTX)

        wanted = listed(across)
        rank = jnp.sum(jnp.where(wanted & (across < down), 1, 0), axis=1, keepdims=True)
        chosen = listed(down) & (jnp.broadcast_to(rank, (32, 128)) == across)
        total = jnp.sum(jnp.where(wanted, 1, 0), axis=1, keepdims=True)
        cut_off = jnp.sum(jnp.where(wanted & (across * half < lo1), 1, 0), axis=1, keepdims=True)
        at_row = jnp.sum(jnp.where(chosen, jnp.broadcast_to(stored_col, (32, 128)), 0), axis=0, keepdims=True)
        p_row = jnp.sum(jnp.where(chosen, down, 0), axis=0, keepdims=True)
        lane1 = across[0:1]
        plan_ref[20 + 2 * i:21 + 2 * i, :] = jnp.where(lane1 == 64, total[0:1], at_row)
        plan_ref[21 + 2 * i:22 + 2 * i, :] = jnp.where(lane1 == 64, cut_off[0:1], p_row)


    keep.wait()
    q_copy.wait()
    low = slots[2 * ctx]
    high = slots[2 * ctx + 1]
    k_own = jnp.concatenate([low[:, :64], high[:, :64]], axis=1)
    v_own = jnp.concatenate([low[:, 64:], high[:, 64:]], axis=1)
    heads = q_ref.shape[1] // DH
    key = lax.broadcasted_iota(jnp.int32, (half, DIAG), 1)
    row = lax.broadcasted_iota(jnp.int32, (half, DIAG), 0)
    for i in range(2):
        begin = i * (rows - DIAG)
        first = own_ref[i] * half
        lo = jnp.zeros((half, DIAG), jnp.int32)
        for cut in cuts:
            lo = jnp.where(cut <= first + row, jnp.maximum(lo, cut), lo)
        at = key + begin - i * half
        allowed = (at >= 0) & (at <= row) & (first + at >= lo)
        k = k_own[begin:begin + DIAG]
        v = v_own[begin:begin + DIAG]
        k_self = k_own[i * half:(i + 1) * half].astype(jnp.float32)
        for h in range(heads):
            q = q_ref[i * half:(i + 1) * half, h * DH:(h + 1) * DH]
            m = jnp.sum(q.astype(jnp.float32) * k_self, axis=1, keepdims=True) * SCALE
            s = lax.dot_general(q, k, NT, preferred_element_type=jnp.float32) * SCALE - m
            p = jnp.exp2(jnp.where(allowed, s, NEG))
            mx[i * heads + h] = jnp.broadcast_to(m, (half, DH))
            tot[i * heads + h] = p[:, :DH] + p[:, DH:]
            acc[i * heads + h] = jnp.dot(p.astype(jnp.bfloat16), v, preferred_element_type=jnp.float32)

    for da in DIM2[1:]:
        spread(da)
    for da in DIM2:
        if da != 2:
            wait(("++", da))
            wait(("--", da))
        else:
            wait(("2", da))
        share(da, 2)

    def assemble(place, which):
        c = place * 2 + which
        at = pl.ds(pl.multiple_of(c * rows, rows), rows)
        low = slots[2 * c]
        high = slots[2 * c + 1]
        ka_ref[at, :] = jnp.concatenate([low[:, :64], high[:, :64]], axis=1)
        va_ref[at, :] = jnp.concatenate([low[:, 64:], high[:, 64:]], axis=1)

    for place in range(N_CTX // 2):
        assemble(place, core)
    for index, da, db in shared:
        sib(index, da, db, True).wait_recv()
    for place in range(N_CTX // 2):
        assemble(place, 1 - core)
    for cp in started:
        cp.wait_send()


def gather(own, ids, k, v, q):
    rows = k.shape[0]
    vm = pl.BlockSpec(memory_space=pltpu.VMEM)
    hbm = pl.BlockSpec(memory_space=pltpu.HBM)
    n = 3 + 2 * len(DIM2) + 2 * (len(DIM2) - 1) + 1
    every = jax.ShapeDtypeStruct((N_CTX * rows, 128), jnp.bfloat16)
    state = jax.ShapeDtypeStruct((2 * (q.shape[1] // DH), rows // 2, DH), jnp.float32)
    return pl.pallas_call(
        gather_kernel,
        out_shape=(every, every, jax.ShapeDtypeStruct((24, 128), jnp.int32),
                   jax.ShapeDtypeStruct(q.shape, q.dtype), state, state, state),
        in_specs=[hbm] * 5,
        out_specs=(vm,) * 7,
        scratch_shapes=[
            pltpu.VMEM((2 * N_CTX, rows, 128), jnp.bfloat16),
            pltpu.VMEM((128, rows), jnp.bfloat16),
            pltpu.SMEM((2,), jnp.int32),
            pltpu.VMEM((3, 128), jnp.int32),
            pltpu.SemaphoreType.DMA((5,)),
            pltpu.VMEM((rows, 128), jnp.bfloat16),
            pltpu.VMEM((N_CTX, 8, 128), jnp.int32),
            pltpu.SemaphoreType.DMA((n,)),
            pltpu.SemaphoreType.DMA((n,)),
            pltpu.SemaphoreType.DMA((16,)),
            pltpu.SemaphoreType.DMA((16,)),
            pltpu.SemaphoreType.DMA((N_CTX,)),
            pltpu.SemaphoreType.DMA((N_CTX,)),
            pltpu.SemaphoreType.DMA(()),
        ],
        compiler_params=pltpu.CompilerParams(
            collective_id=0, has_side_effects=True, vmem_limit_bytes=24 * 2**20),
        name="gather",
    )(*(pltpu.with_memory_space_constraint(x, pltpu.HBM) for x in (own, ids.reshape(3, 128), k.T, v.T, q)))


DH = 128
HALF = 192
NBLK = 32
SEQ = 6144
LOG2E = 1.4426950408889634
SCALE = DH ** -0.5 * LOG2E
NEG = -1e30
LIMIT = 2.0 ** 100
EDGE = 2
NT = (((1,), (1,)), ((), ()))


def attend_kernel(plan_ref, q_ref, k_ref, v_ref, acc_in, tot_in, mx_in, o_hbm,
                  acc, tot, o_ref, sem):
    heads = q_ref.shape[1] // DH
    ctx = lax.axis_index("ctx")
    cuts = [plan_ref[16 + cut, 0] for cut in range(3)]

    def start_of(pos):
        lo = jnp.zeros_like(pos)
        for cut in cuts:
            lo = jnp.where(cut <= pos, jnp.maximum(lo, cut), lo)
        return lo

    def rows_of(p):
        return pl.ds(pl.multiple_of(plan_ref[19, p] * HALF, HALF), HALF)

    def gathered(ref, places):
        return jnp.concatenate(
            [ref[pl.ds(pl.multiple_of(at * HALF, HALF), HALF), :] for at in places], axis=0)

    for i in range(2):
        block = plan_ref[ctx, i]
        first = block * HALF
        lo0 = start_of(first)
        head = lo0 // HALF
        total = plan_ref[20 + 2 * i, 64]
        n_edge = plan_ref[21 + 2 * i, 64]
        n_edge = n_edge + (total - n_edge) % WIDE
        rows = slice(i * HALF, (i + 1) * HALF)
        for h in range(heads):
            acc[h] = acc_in[i * heads + h]
            tot[h] = tot_in[i * heads + h]
        qpos = first + lax.broadcasted_iota(jnp.int32, (HALF, HALF), 0)
        lo_rows = start_of(qpos)
        lane = lax.broadcasted_iota(jnp.int32, (HALF, HALF), 1)
        wide_lo = start_of(first + lax.broadcasted_iota(jnp.int32, (HALF, EDGE * HALF), 0))
        wide_lane = lax.broadcasted_iota(jnp.int32, (HALF, EDGE * HALF), 1)

        def edge_blocks(t):
            index = [EDGE * t + e for e in range(EDGE)]
            index = [jnp.minimum(at, 63) for at in index]
            blocks = [plan_ref[21 + 2 * i, at] for at in index]
            kpos = None
            for e, (at, p) in enumerate(zip(index, blocks)):
                here = jnp.where(at < n_edge, p * HALF - HALF * e, -SEQ) + wide_lane
                kpos = here if kpos is None else jnp.where(wide_lane < HALF * e, kpos, here)
            return [plan_ref[20 + 2 * i, at] for at in index], kpos >= wide_lo

        def step(blocks, allowed):
            k = gathered(k_ref, blocks)
            v = gathered(v_ref, blocks)
            wide = HALF * len(blocks)

            def scores(h):
                return lax.dot_general(q_ref[rows, h * DH:(h + 1) * DH], k, NT,
                                       preferred_element_type=jnp.float32)

            nxt = scores(0)
            for h in range(heads):
                s = nxt
                if h + 1 < heads:
                    nxt = scores(h + 1)
                s = s * SCALE - jnp.concatenate([mx_in[i * heads + h]] * (wide // DH), axis=1)
                if allowed is not None:
                    s = jnp.where(allowed, s, NEG)
                p = jnp.exp2(s)
                t = tot[h]
                for part in range(wide // DH):
                    t = t + p[:, part * DH:(part + 1) * DH]
                tot[h] = t
                acc[h] += jnp.dot(p.astype(jnp.bfloat16), v, preferred_element_type=jnp.float32)

        def edge(t, _):
            step(*edge_blocks(t))
            return 0

        def inner(t, _):
            step([plan_ref[20 + 2 * i, n_edge + WIDE * t + e] for e in range(WIDE)], None)
            return 0

        n_steps = (n_edge + EDGE - 1) // EDGE
        lax.fori_loop(0, n_steps, edge, 0)
        lax.fori_loop(0, (total - n_edge) // WIDE, inner, 0)

        worst = None
        for h in range(heads):
            t = jnp.sum(tot[h], axis=1, keepdims=True)
            worst = t if worst is None else jnp.maximum(worst, t)
            o_ref[rows, h * DH:(h + 1) * DH] = (acc[h] * (1.0 / t)).astype(jnp.bfloat16)

        @pl.when(jnp.logical_not(jnp.max(worst) < LIMIT))
        def _():
            def one(h, _):
                cols = pl.ds(pl.multiple_of(h * DH, DH), DH)
                q = q_ref[rows, cols]

                def safe(p, carry):
                    top, total, mixed = carry
                    s = lax.dot_general(q, k_ref[rows_of(p), :], NT, preferred_element_type=jnp.float32) * SCALE
                    kpos = p * HALF + lane
                    ok = (kpos <= qpos) & (kpos >= lo_rows)
                    s = jnp.where(ok, s, NEG)
                    new = jnp.maximum(top, jnp.max(s, axis=1, keepdims=True))
                    w = jnp.where(ok, jnp.exp2(s - new), 0.0)
                    fade = jnp.exp2(top - new)
                    total = total * fade + jnp.sum(w, axis=1, keepdims=True)
                    mixed = mixed * fade + jnp.dot(w.astype(jnp.bfloat16), v_ref[rows_of(p), :],
                                                   preferred_element_type=jnp.float32)
                    return new, total, mixed

                top, total, mixed = lax.fori_loop(
                    head, block + 1, safe,
                    (jnp.full((HALF, 1), NEG, jnp.float32), jnp.zeros((HALF, 1), jnp.float32),
                     jnp.zeros((HALF, DH), jnp.float32)))
                o_ref[rows, cols] = (mixed / total).astype(jnp.bfloat16)
                return 0

            lax.fori_loop(0, heads, one, 0)

        pltpu.make_async_copy(o_ref.at[rows], o_hbm.at[rows], sem.at[i]).start()

    for i in range(2):
        rows = slice(i * HALF, (i + 1) * HALF)
        pltpu.make_async_copy(o_ref.at[rows], o_hbm.at[rows], sem.at[i]).wait()


def attend(plan, q, k, v, acc, tot, mx):
    heads = q.shape[1] // DH
    vm = pl.BlockSpec(memory_space=pltpu.VMEM)
    sm = pl.BlockSpec(memory_space=pltpu.SMEM)
    hbm = pl.BlockSpec(memory_space=pltpu.HBM)
    return pl.pallas_call(
        attend_kernel,
        out_shape=jax.ShapeDtypeStruct(q.shape, jnp.bfloat16),
        in_specs=[sm] + [vm] * 6,
        out_specs=hbm,
        scratch_shapes=[
            pltpu.VMEM((heads, HALF, DH), jnp.float32),
            pltpu.VMEM((heads, HALF, DH), jnp.float32),
            pltpu.VMEM(q.shape, jnp.bfloat16),
            pltpu.SemaphoreType.DMA((2,)),
        ],
        compiler_params=pltpu.CompilerParams(vmem_limit_bytes=32 * 2**20),
        name="attend",
    )(plan, q, k, v, acc, tot, mx)


def per_device(query_rows, key_rows, value_rows, block_order, rollout_ids):
    keys, values, plan, query, acc, tot, mx = gather(
        block_order, rollout_ids, key_rows, value_rows, query_rows)
    return attend(plan, query, keys, values, acc, tot, mx)


def solution(mesh):
    return jax.shard_map(
        per_device,
        mesh=mesh,
        in_specs=(P("ctx", "head"), P("ctx", "head"), P("ctx", "head"), P("ctx"), P("ctx")),
        out_specs=P("ctx", "head"),
        check_vma=False,
    )
```
